32 devices in a mesh: rep: 8 (over y, x, core), fsdp: 4 (over z).
Axes of the slice: x: 2, y: 2, z: 4, core: 2. Of those that a mesh axis runs over, the one named last changes fastest.
Arguments:
- activations: bfloat16 [8192, 4096], P('rep', 'fsdp'), may hold values from -6 to 6
- cotangent: bfloat16 [8192, 512], P(('rep', 'fsdp')), may hold values from -6 to 6
- token_ids: int32 [8192], P(('rep', 'fsdp')), may hold values from 0 to 31999, as said below
- round_index: int32 [], replicated, may hold values from 0 to 2
- master_weight: float32 [8, 4096, 512], P('rep', 'fsdp'), may hold values from -0.09375 to 0.09375
- first_moment: float32 [8, 4096, 512], P('rep', 'fsdp'), may hold values from -0.4375 to 0.4375
- second_moment: float32 [8, 4096, 512], P('rep', 'fsdp'), may hold values from 5e-05 to 0.0005
Outputs:
- input_grad: bfloat16 [8192, 4096], P('rep', 'fsdp')
- blended_weight: float32 [8, 4096, 512], P('rep', 'fsdp')
- blended_moment: float32 [8, 4096, 512], P('rep', 'fsdp')
- new_second: float32 [8, 4096, 512], P('rep', 'fsdp')
The draws below stay inside these ranges and needn't reach their ends.
Inputs may be any that keep to these rules, and one draw needn't show every extreme that they name: `token_ids`: id 0 marks padding; other ids are tokens of a vocabulary of 32000.
All inputs are finite; a program needn't handle non-finite values.
Results may differ from the reference program's by a relative error of at most 0.005.
Values may be sent and summed in bfloat16 or wider, within the bound.
A program may use at most 64 MiB of HBM per device.

```python
import math
import jax
import jax.numpy as jnp
from jax import lax

DIN = 4096
KVW = 512
VOCAB = 32000
TOK_REP = 1024
REPS = 8
TOKENS = 8192
LOG_REP = 3
N_REP = 8


def draw_token_ids(key, part):
    key = jax.random.fold_in(key, 7)
    first_key, second_key = jax.random.split(key)
    words = jax.random.randint(first_key, (TOKENS,), 1, VOCAB)
    padding = jax.random.randint(second_key, (TOKENS,), 0, 4)
    return jnp.where(padding == 0, 0, words).astype(jnp.int32)


def shard_levels(rng, shape, cuts, low, largest):
    level = 1.0
    for position, parts in cuts:
        draws = jax.random.uniform(jax.random.fold_in(jax.random.fold_in(rng, 6), position), (parts,), jnp.float32, low / len(cuts), largest / len(cuts))
        level = level * jnp.repeat(jnp.exp(draws), shape[position] // parts).reshape((-1,) + (1,) * (len(shape) - 1 - position))
    return level


def centred(key, shape, scale, most, cuts=(), held_as=jnp.bfloat16):
    values = jax.random.normal(key, shape, jnp.float32) * scale
    if len(cuts) > 0:
        values = shard_levels(key, shape, cuts, -0.22, 0.18) * values
    return jnp.clip(values, min=-most, max=most).astype(held_as)


def setup_inputs(seed: int = 0) -> dict:
    arg_keys = jax.random.split(jax.random.key(seed), 8)
    activations = centred(arg_keys[0], (TOKENS, DIN), 1.0, 6.0, ((0, 8), (1, 4)))
    cotangent = centred(arg_keys[1], (TOKENS, KVW), 1.0, 6.0, ((0, 32),))
    token_ids = draw_token_ids(jax.random.fold_in(arg_keys[7], 71), 0)
    round_index = jax.random.randint(arg_keys[3], (), 0, LOG_REP).astype(jnp.int32)
    master_weight = centred(arg_keys[4], (REPS, DIN, KVW), DIN ** -0.5, 0.09375, ((0, 8), (1, 4)), jnp.float32)
    first_moment = centred(arg_keys[5], (REPS, DIN, KVW), 0.03, 0.4375, ((0, 8), (1, 4)), jnp.float32)
    second_moment = jnp.clip(jnp.exp(math.log(0.0005) - 2.3025852 * jax.random.uniform(arg_keys[6], (REPS, DIN, KVW), jnp.float32) ** shard_levels(arg_keys[6], (REPS, DIN, KVW), ((0, 8), (1, 4)), -0.2, 0.2)), 4.999999873689376e-05, 0.0005)
    return {"activations": activations, "cotangent": cotangent, "token_ids": token_ids, "round_index": round_index, "master_weight": master_weight, "first_moment": first_moment, "second_moment": second_moment}


learn_rate = 0.002
beta_one = 0.9
beta_two = 0.95
epsilon = 1e-08
decay_rate = 0.1

def reference(activations, cotangent, token_ids, round_index, master_weight, first_moment, second_moment):
    keep_rows = token_ids != 0
    masked = jnp.where(keep_rows[:, None], cotangent, jnp.zeros_like(cotangent))
    by_replica = activations.reshape(N_REP, TOK_REP, DIN)
    cot_replica = masked.reshape(N_REP, TOK_REP, KVW)

    def replica_step(inputs):
        local_inputs, local_cotangent, local_weight = inputs
        gradient = jnp.dot(local_inputs.T, local_cotangent, preferred_element_type=jnp.float32) / TOK_REP
        result = jnp.dot(local_cotangent, local_weight.astype(jnp.bfloat16).T, preferred_element_type=jnp.float32).astype(jnp.bfloat16)
        return (gradient, result)
    gradient, result = lax.map(replica_step, (by_replica, cot_replica, master_weight))
    input_grad = result.reshape(TOKENS, DIN)
    new_moment = beta_one * first_moment + (1.0 - beta_one) * gradient
    new_second = beta_two * second_moment + (1.0 - beta_two) * gradient * gradient
    updated = master_weight - learn_rate * (new_moment / (jnp.sqrt(new_second) + epsilon) + decay_rate * master_weight)
    offset = jnp.left_shift(jnp.int32(1), round_index.astype(jnp.int32)) % N_REP
    blended_weight = 0.5 * (updated + jnp.roll(updated, offset, axis=0))
    blended_moment = 0.5 * (new_moment + jnp.roll(new_moment, offset, axis=0))
    return (input_grad, blended_weight, blended_moment, new_second)
```

```python
from functools import partial

import jax
import jax.numpy as jnp
from jax import lax
from jax.experimental import pallas as pl
from jax.experimental.pallas import tpu as pltpu
from jax.sharding import PartitionSpec as P

learn_rate = 0.002
beta_one = 0.9
beta_two = 0.95
epsilon = 1e-08
decay_rate = 0.1

MESH = pl.DeviceIdType.MESH
WIDE = 128
TALL = 256


def body(
    replicas,
    shards,
    offset,
    acts_hbm,
    cot_hbm,
    ids_ref,
    weight_hbm,
    moment_hbm,
    second_hbm,
    grad_hbm,
    out_weight_hbm,
    out_moment_hbm,
    out_second_hbm,
    acts,
    acts_t,
    cot,
    gath,
    weight,
    moment,
    second,
    weight_half,
    grad,
    outbox,
    inbox,
    load_sem,
    store_sem,
    second_sem,
    grad_sem,
    gather_send,
    gather_recv,
    gossip_send,
    gossip_recv,
):
    rep = lax.axis_index("rep")
    shard = lax.axis_index("fsdp")
    rows, width = cot.shape
    tokens, feats = acts.shape
    chunks = width // WIDE
    tall = min(TALL, feats)
    pieces = feats // tall

    loads = [
        pltpu.make_async_copy(cot_hbm, cot, load_sem.at[0]),
        pltpu.make_async_copy(acts_hbm, acts, load_sem.at[1]),
        pltpu.make_async_copy(weight_hbm.at[0], weight, load_sem.at[2]),
        pltpu.make_async_copy(moment_hbm.at[0], moment, load_sem.at[3]),
        pltpu.make_async_copy(second_hbm.at[0], second, load_sem.at[4]),
    ]
    for load in loads:
        load.start()

    target = lax.rem(rep + offset, replicas)
    source = lax.rem(rep + replicas - offset, replicas)
    barrier = pltpu.get_barrier_semaphore()
    for j in range(1, shards):
        peer = lax.rem(shard + j, shards)
        pl.semaphore_signal(barrier, inc=1, device_id=(rep, peer), device_id_type=MESH)
    pl.semaphore_signal(barrier, inc=1, device_id=(target, shard), device_id_type=MESH)
    signals = shards
    if (2 * offset) % replicas != 0:
        pl.semaphore_signal(barrier, inc=1, device_id=(source, shard), device_id_type=MESH)
        signals += 1

    keep = jnp.where(ids_ref[...] != 0, 1.0, 0.0).astype(jnp.float32)
    keep = jnp.broadcast_to(keep, (WIDE, rows)).T
    mine = pl.ds(pl.multiple_of(shard * rows, rows), rows)
    loads[0].wait()
    for c in range(chunks):
        part = cot[:, c * WIDE : (c + 1) * WIDE].astype(jnp.float32)
        gath[c, mine, :] = jnp.where(keep != 0.0, part, 0.0).astype(jnp.bfloat16)

    def gather_copy(c, j):
        peer = lax.rem(shard + j, shards)
        return pltpu.make_async_remote_copy(
            src_ref=gath.at[c, mine, :],
            dst_ref=gath.at[c, mine, :],
            send_sem=gather_send.at[c, j - 1],
            recv_sem=gather_recv.at[c, j - 1],
            device_id=(rep, peer),
            device_id_type=MESH,
        )

    def gather_wait(c):
        for j in range(1, shards):
            peer = lax.rem(shard + shards - j, shards)
            theirs = pl.ds(pl.multiple_of(peer * rows, rows), rows)
            pltpu.make_async_remote_copy(
                src_ref=gath.at[c, theirs, :],
                dst_ref=gath.at[c, theirs, :],
                send_sem=gather_send.at[c, j - 1],
                recv_sem=gather_recv.at[c, j - 1],
                device_id=(rep, peer),
                device_id_type=MESH,
            ).wait_recv()

    def gossip_copy(c, p):
        return pltpu.make_async_remote_copy(
            src_ref=outbox.at[c, p],
            dst_ref=inbox.at[c, p],
            send_sem=gossip_send.at[c, p],
            recv_sem=gossip_recv.at[c, p],
            device_id=(target, shard),
            device_id_type=MESH,
        )

    pl.semaphore_wait(barrier, signals)
    for j in range(1, shards):
        gather_copy(0, j).start()

    loads[1].wait()

    @pl.loop(0, pieces)
    def _(p):
        span = pl.ds(pl.multiple_of(p * tall, tall), tall)
        acts_t[span, :] = acts[:, span].T

    loads[2].wait()
    weight_half[...] = weight[...].astype(jnp.bfloat16)
    loads[3].wait()
    loads[4].wait()

    for c in range(chunks):
        gather_wait(c)
        if c + 1 < chunks:
            for j in range(1, shards):
                gather_copy(c + 1, j).start()
        columns = slice(c * WIDE, (c + 1) * WIDE)

        @pl.loop(0, pieces)
        def _(p):
            span = pl.ds(pl.multiple_of(p * tall, tall), tall)
            gradient = jnp.dot(
                acts_t[span, :], gath[c], preferred_element_type=jnp.float32
            ) * (1.0 / tokens)
            own = weight[span, columns]
            new_moment = beta_one * moment[span, columns] + (1.0 - beta_one) * gradient
            new_second = beta_two * second[span, columns] + (1.0 - beta_two) * gradient * gradient
            updated = own - learn_rate * (
                new_moment / (jnp.sqrt(new_second) + epsilon) + decay_rate * own
            )
            outbox[c, p, 0] = updated.astype(jnp.bfloat16)
            outbox[c, p, 1] = new_moment.astype(jnp.bfloat16)
            gossip_copy(c, p).start()
            weight[span, columns] = updated
            moment[span, columns] = new_moment
            second[span, columns] = new_second

    pltpu.make_async_copy(second, out_second_hbm.at[0], second_sem).start()

    gtall = min(TALL, tokens)

    @pl.loop(0, tokens // gtall)
    def _(t):
        span = pl.ds(pl.multiple_of(t * gtall, gtall), gtall)
        left = jnp.concatenate([gath[c, span, :] for c in range(chunks)], axis=1)
        grad[span, :] = lax.dot_general(
            left, weight_half[...], (((1,), (1,)), ((), ())), preferred_element_type=jnp.float32
        ).astype(jnp.bfloat16)

    pltpu.make_async_copy(grad, grad_hbm, grad_sem).start()

    def stores(c, p):
        span = pl.ds(pl.multiple_of(p * tall, tall), tall)
        columns = pl.ds(c * WIDE, WIDE)
        return (
            pltpu.make_async_copy(
                weight.at[span, columns], out_weight_hbm.at[0, span, columns], store_sem.at[0, c, p]
            ),
            pltpu.make_async_copy(
                moment.at[span, columns], out_moment_hbm.at[0, span, columns], store_sem.at[1, c, p]
            ),
        )

    for c in range(chunks):
        columns = slice(c * WIDE, (c + 1) * WIDE)

        @pl.loop(0, pieces)
        def _(p):
            span = pl.ds(pl.multiple_of(p * tall, tall), tall)
            gossip_copy(c, p).wait_recv()
            weight[span, columns] = 0.5 * (weight[span, columns] + inbox[c, p, 0].astype(jnp.float32))
            moment[span, columns] = 0.5 * (moment[span, columns] + inbox[c, p, 1].astype(jnp.float32))
            for store in stores(c, p):
                store.start()

    for c in range(chunks):
        for j in range(1, shards):
            gather_copy(c, j).wait_send()

        @pl.loop(0, pieces)
        def _(p):
            gossip_copy(c, p).wait_send()
            for store in stores(c, p):
                store.wait()

    pltpu.make_async_copy(second, out_second_hbm.at[0], second_sem).wait()
    pltpu.make_async_copy(grad, grad_hbm, grad_sem).wait()


def fused(replicas, shards, level, acts, cot, ids, weight, moment, second):
    tokens, feats = acts.shape
    rows, width = cot.shape
    chunks = width // WIDE
    tall = min(TALL, feats)
    pieces = feats // tall
    state = jax.ShapeDtypeStruct(weight.shape, jnp.float32)
    anywhere = pl.BlockSpec(memory_space=pl.ANY)
    return pl.pallas_call(
        partial(body, replicas, shards, (1 << level) % replicas),
        out_shape=(jax.ShapeDtypeStruct((tokens, feats), jnp.bfloat16), state, state, state),
        in_specs=[
            anywhere,
            anywhere,
            pl.BlockSpec(memory_space=pltpu.VMEM),
            anywhere,
            anywhere,
            anywhere,
        ],
        out_specs=(anywhere,) * 4,
        scratch_shapes=[
            pltpu.VMEM((tokens, feats), jnp.bfloat16),
            pltpu.VMEM((feats, tokens), jnp.bfloat16),
            pltpu.VMEM((rows, width), jnp.bfloat16),
            pltpu.VMEM((chunks, tokens, WIDE), jnp.bfloat16),
            pltpu.VMEM((feats, width), jnp.float32),
            pltpu.VMEM((feats, width), jnp.float32),
            pltpu.VMEM((feats, width), jnp.float32),
            pltpu.VMEM((feats, width), jnp.bfloat16),
            pltpu.VMEM((tokens, feats), jnp.bfloat16),
            pltpu.VMEM((chunks, pieces, 2, tall, WIDE), jnp.bfloat16),
            pltpu.VMEM((chunks, pieces, 2, tall, WIDE), jnp.bfloat16),
            pltpu.SemaphoreType.DMA((5,)),
            pltpu.SemaphoreType.DMA((2, chunks, pieces)),
            pltpu.SemaphoreType.DMA,
            pltpu.SemaphoreType.DMA,
            pltpu.SemaphoreType.DMA((chunks, shards - 1)),
            pltpu.SemaphoreType.DMA((chunks, shards - 1)),
            pltpu.SemaphoreType.DMA((chunks, pieces)),
            pltpu.SemaphoreType.DMA((chunks, pieces)),
        ],
        compiler_params=pltpu.CompilerParams(
            collective_id=level, has_side_effects=True, vmem_limit_bytes=48 * 1024 * 1024
        ),
        name=f"gossip_offset_{1 << level}",
    )(acts, cot, ids, weight, moment, second)


def on_device(replicas, shards, acts, cot, token_ids, round_index, weight, moment, second):
    levels = max(1, replicas.bit_length() - 1)
    branches = [partial(fused, replicas, shards, level) for level in range(levels)]
    ids = token_ids.reshape(1, -1)
    return lax.switch(round_index, branches, acts, cot, ids, weight, moment, second)


def solution(mesh):
    return jax.shard_map(
        partial(on_device, mesh.shape["rep"], mesh.shape["fsdp"]),
        mesh=mesh,
        in_specs=(
            P("rep", "fsdp"),
            P(("rep", "fsdp"), None),
            P(("rep", "fsdp")),
            P(),
            P("rep", "fsdp", None),
            P("rep", "fsdp", None),
            P("rep", "fsdp", None),
        ),
        out_specs=(
            P("rep", "fsdp"),
            P("rep", "fsdp", None),
            P("rep", "fsdp", None),
            P("rep", "fsdp", None),
        ),
        check_vma=False,
    )
```

```python
from functools import partial

import jax
import jax.numpy as jnp
from jax import lax
from jax.experimental import pallas as pl
from jax.experimental.pallas import tpu as pltpu
from jax.sharding import PartitionSpec as P

learn_rate = 0.002
beta_one = 0.9
beta_two = 0.95
epsilon = 1e-08
decay_rate = 0.1

MESH = pl.DeviceIdType.MESH
WIDE = 128
PARTS = 4
TALL = 256


def body(
    replicas,
    shards,
    offset,
    acts_hbm,
    cot_hbm,
    ids_ref,
    weight_hbm,
    moment_hbm,
    second_hbm,
    grad,
    weight_out,
    moment_out,
    second_out,
    acts,
    acts_t,
    cot,
    gath,
    weight_half,
    outbox,
    inbox,
    load_sem,
    state_sem,
    gather_send,
    gather_recv,
    gossip_send,
    gossip_recv,
):
    rep = lax.axis_index("rep")
    shard = lax.axis_index("fsdp")
    rows, width = cot.shape
    tokens, feats = acts.shape
    chunks = width // WIDE
    tall = min(TALL, feats)
    pieces = feats // tall
    weight, moment, second = weight_out.at[0], moment_out.at[0], second_out.at[0]

    def state_loads(c):
        columns = pl.ds(c * WIDE, WIDE)
        return [
            pltpu.make_async_copy(far.at[0, :, columns], near.at[:, columns], state_sem.at[i, c])
            for i, (far, near) in enumerate(
                ((weight_hbm, weight), (moment_hbm, moment), (second_hbm, second))
            )
        ]

    cot_load = pltpu.make_async_copy(cot_hbm, cot, load_sem.at[0])
    acts_load = pltpu.make_async_copy(acts_hbm, acts, load_sem.at[1])
    cot_load.start()

    target = lax.rem(rep + offset, replicas)
    source = lax.rem(rep + replicas - offset, replicas)
    barrier = pltpu.get_barrier_semaphore()
    for j in range(1, shards):
        peer = lax.rem(shard + j, shards)
        pl.semaphore_signal(barrier, inc=1, device_id=(rep, peer), device_id_type=MESH)
    pl.semaphore_signal(barrier, inc=1, device_id=(target, shard), device_id_type=MESH)
    signals = shards
    if (2 * offset) % replicas != 0:
        pl.semaphore_signal(barrier, inc=1, device_id=(source, shard), device_id_type=MESH)
        signals += 1

    acts_load.start()
    for c in range(chunks):
        for load in state_loads(c):
            load.start()

    keep = jnp.where(ids_ref[...] != 0, 1.0, 0.0).astype(jnp.float32)
    keep = jnp.broadcast_to(keep, (WIDE, rows)).T
    mine = pl.ds(pl.multiple_of(shard * rows, rows), rows)

    def mask(c):
        part = cot[:, c * WIDE : (c + 1) * WIDE].astype(jnp.float32)
        gath[c, mine, :] = jnp.where(keep != 0.0, part, 0.0).astype(jnp.bfloat16)

    cot_load.wait()
    mask(0)

    def gather_copy(c, j):
        peer = lax.rem(shard + j, shards)
        return pltpu.make_async_remote_copy(
            src_ref=gath.at[c, mine, :],
            dst_ref=gath.at[c, mine, :],
            send_sem=gather_send.at[c, j - 1],
            recv_sem=gather_recv.at[c, j - 1],
            device_id=(rep, peer),
            device_id_type=MESH,
        )

    def gather_wait(c):
        for j in range(1, shards):
            peer = lax.rem(shard + shards - j, shards)
            theirs = pl.ds(pl.multiple_of(peer * rows, rows), rows)
            pltpu.make_async_remote_copy(
                src_ref=gath.at[c, theirs, :],
                dst_ref=gath.at[c, theirs, :],
                send_sem=gather_send.at[c, j - 1],
                recv_sem=gather_recv.at[c, j - 1],
                device_id=(rep, peer),
                device_id_type=MESH,
            ).wait_recv()

    def gossip_copy(c, p):
        return pltpu.make_async_remote_copy(
            src_ref=outbox.at[c, p],
            dst_ref=inbox.at[c, p],
            send_sem=gossip_send.at[c, p],
            recv_sem=gossip_recv.at[c, p],
            device_id=(target, shard),
            device_id_type=MESH,
        )

    pl.semaphore_wait(barrier, signals)
    for j in range(1, shards):
        gather_copy(0, j).start()

    for c in range(1, chunks):
        mask(c)
    acts_load.wait()

    @pl.loop(0, pieces)
    def _(p):
        span = pl.ds(pl.multiple_of(p * tall, tall), tall)
        acts_t[span, :] = acts[:, span].T

    for c in range(chunks):
        for j in range(1, shards):
            gather_copy(c, j).wait_send()
            if c + 1 < chunks:
                gather_copy(c + 1, j).start()
        for load in state_loads(c):
            load.wait()
        gather_wait(c)
        columns = slice(c * WIDE, (c + 1) * WIDE)

        @pl.loop(0, pieces)
        def _(p):
            span = pl.ds(pl.multiple_of(p * tall, tall), tall)
            gradient = jnp.dot(
                acts_t[span, :], gath[c], preferred_element_type=jnp.float32
            ) * (1.0 / tokens)
            own = weight[span, columns]
            new_moment = beta_one * moment[span, columns] + (1.0 - beta_one) * gradient
            new_second = beta_two * second[span, columns] + (1.0 - beta_two) * gradient * gradient
            updated = own - learn_rate * (
                new_moment / (jnp.sqrt(new_second) + epsilon) + decay_rate * own
            )
            outbox[c, p, 0] = updated.astype(jnp.bfloat16)
            outbox[c, p, 1] = new_moment.astype(jnp.bfloat16)
            gossip_copy(c, p).start()
            weight_half[span, columns] = own.astype(jnp.bfloat16)
            weight[span, columns] = updated
            moment[span, columns] = new_moment
            second[span, columns] = new_second

    gtall = min(TALL, tokens)

    @pl.loop(0, tokens // gtall)
    def _(t):
        span = pl.ds(pl.multiple_of(t * gtall, gtall), gtall)
        left = jnp.concatenate([gath[c, span, :] for c in range(chunks)], axis=1)
        grad[span, :] = lax.dot_general(
            left, weight_half[...], (((1,), (1,)), ((), ())), preferred_element_type=jnp.float32
        ).astype(jnp.bfloat16)

    for c in range(chunks):
        columns = slice(c * WIDE, (c + 1) * WIDE)

        @pl.loop(0, pieces)
        def _(p):
            span = pl.ds(pl.multiple_of(p * tall, tall), tall)
            gossip_copy(c, p).wait_recv()
            weight[span, columns] = 0.5 * (weight[span, columns] + inbox[c, p, 0].astype(jnp.float32))
            moment[span, columns] = 0.5 * (moment[span, columns] + inbox[c, p, 1].astype(jnp.float32))

    for c in range(chunks):

        @pl.loop(0, pieces)
        def _(p):
            gossip_copy(c, p).wait_send()


def settle(values):
    def write(*refs):
        count = len(values)
        sem = refs[-1]
        copies = []
        for i in range(count):
            rows = values[i].shape[-2] // PARTS
            for part in range(PARTS):
                span = pl.ds(part * rows, rows)
                index = (span, slice(None)) if values[i].ndim == 2 else (0, span, slice(None))
                copies.append(
                    pltpu.make_async_copy(
                        refs[i].at[index], refs[count + i].at[index], sem.at[i, part]
                    )
                )
        for copy in copies:
            copy.start()
        for copy in copies:
            copy.wait()

    return pl.pallas_call(
        write,
        out_shape=tuple(jax.ShapeDtypeStruct(v.shape, v.dtype) for v in values),
        in_specs=[pl.BlockSpec(memory_space=pltpu.VMEM)] * len(values),
        out_specs=(pl.BlockSpec(memory_space=pltpu.HBM),) * len(values),
        scratch_shapes=[pltpu.SemaphoreType.DMA((len(values), PARTS))],
        compiler_params=pltpu.CompilerParams(vmem_limit_bytes=4 * 1024 * 1024),
        name="settle",
    )(*[pltpu.with_memory_space_constraint(v, pltpu.VMEM) for v in values])


def fused(replicas, shards, level, acts, cot, ids, weight, moment, second):
    tokens, feats = acts.shape
    rows, width = cot.shape
    chunks = width // WIDE
    tall = min(TALL, feats)
    pieces = feats // tall
    state = pltpu.VMEM(weight.shape, jnp.float32)
    far = pl.BlockSpec(memory_space=pltpu.HBM)
    values = pl.pallas_call(
        partial(body, replicas, shards, (1 << level) % replicas),
        out_shape=(pltpu.VMEM((tokens, feats), jnp.bfloat16), state, state, state),
        in_specs=[
            far,
            far,
            pl.BlockSpec(memory_space=pltpu.VMEM),
            far,
            far,
            far,
        ],
        out_specs=(pl.BlockSpec(memory_space=pltpu.VMEM),) * 4,
        scratch_shapes=[
            pltpu.VMEM((tokens, feats), jnp.bfloat16),
            pltpu.VMEM((feats, tokens), jnp.bfloat16),
            pltpu.VMEM((rows, width), jnp.bfloat16),
            pltpu.VMEM((chunks, tokens, WIDE), jnp.bfloat16),
            pltpu.VMEM((feats, width), jnp.bfloat16),
            pltpu.VMEM((chunks, pieces, 2, tall, WIDE), jnp.bfloat16),
            pltpu.VMEM((chunks, pieces, 2, tall, WIDE), jnp.bfloat16),
            pltpu.SemaphoreType.DMA((2,)),
            pltpu.SemaphoreType.DMA((3, chunks)),
            pltpu.SemaphoreType.DMA((chunks, shards - 1)),
            pltpu.SemaphoreType.DMA((chunks, shards - 1)),
            pltpu.SemaphoreType.DMA((chunks, pieces)),
            pltpu.SemaphoreType.DMA((chunks, pieces)),
        ],
        compiler_params=pltpu.CompilerParams(
            collective_id=level, has_side_effects=True, vmem_limit_bytes=32 * 1024 * 1024
        ),
        name=f"gossip_offset_{1 << level}",
    )(acts, cot, ids, weight, moment, second)
    return settle(values)


def on_device(replicas, shards, acts, cot, token_ids, round_index, weight, moment, second):
    levels = max(1, replicas.bit_length() - 1)
    branches = [partial(fused, replicas, shards, level) for level in range(levels)]
    ids = token_ids.reshape(1, -1)
    return lax.switch(round_index, branches, acts, cot, ids, weight, moment, second)


def solution(mesh):
    return jax.shard_map(
        partial(on_device, mesh.shape["rep"], mesh.shape["fsdp"]),
        mesh=mesh,
        in_specs=(
            P("rep", "fsdp"),
            P(("rep", "fsdp"), None),
            P(("rep", "fsdp")),
            P(),
            P("rep", "fsdp", None),
            P("rep", "fsdp", None),
            P("rep", "fsdp", None),
        ),
        out_specs=(
            P("rep", "fsdp"),
            P("rep", "fsdp", None),
            P("rep", "fsdp", None),
            P("rep", "fsdp", None),
        ),
        check_vma=False,
    )
```

```python
from functools import partial

import jax
import jax.numpy as jnp
from jax import lax
from jax.experimental import pallas as pl
from jax.experimental.pallas import tpu as pltpu
from jax.sharding import PartitionSpec as P

learn_rate = 0.002
beta_one = 0.9
beta_two = 0.95
epsilon = 1e-08
decay_rate = 0.1

MESH = pl.DeviceIdType.MESH
WIDE = 128
PARTS = 4
TALL = 256


def body(
    replicas,
    shards,
    offset,
    acts_hbm,
    cot_hbm,
    ids_hbm,
    weight_hbm,
    moment_hbm,
    second_hbm,
    grad,
    weight_out,
    moment_out,
    second_out,
    acts,
    acts_t,
    cot,
    ids,
    gath,
    weight_half,
    outbox,
    inbox,
    load_sem,
    state_sem,
    gather_send,
    gather_recv,
    gossip_send,
    gossip_recv,
):
    rep = lax.axis_index("rep")
    shard = lax.axis_index("fsdp")
    rows, width = cot.shape
    tokens, feats = acts.shape
    chunks = width // WIDE
    tall = min(TALL, feats)
    pieces = feats // tall
    weight, moment, second = weight_out.at[0], moment_out.at[0], second_out.at[0]

    def state_loads(c):
        columns = pl.ds(c * WIDE, WIDE)
        return [
            pltpu.make_async_copy(far.at[0, :, columns], near.at[:, columns], state_sem.at[i, c])
            for i, (far, near) in enumerate(
                ((weight_hbm, weight), (moment_hbm, moment), (second_hbm, second))
            )
        ]

    cot_load = pltpu.make_async_copy(cot_hbm, cot, load_sem.at[0])
    ids_load = pltpu.make_async_copy(ids_hbm, ids, load_sem.at[2])
    acts_load = pltpu.make_async_copy(acts_hbm, acts, load_sem.at[1])
    ids_load.start()
    cot_load.start()
    target = lax.rem(rep + offset, replicas)
    source = lax.rem(rep + replicas - offset, replicas)
    barrier = pltpu.get_barrier_semaphore()
    for j in range(1, shards):
        peer = lax.rem(shard + j, shards)
        pl.semaphore_signal(barrier, inc=1, device_id=(rep, peer), device_id_type=MESH)
    pl.semaphore_signal(barrier, inc=1, device_id=(target, shard), device_id_type=MESH)
    signals = shards
    if (2 * offset) % replicas != 0:
        pl.semaphore_signal(barrier, inc=1, device_id=(source, shard), device_id_type=MESH)
        signals += 1

    acts_load.start()
    for c in range(chunks):
        for load in state_loads(c):
            load.start()

    ids_load.wait()
    keep = jnp.where(ids[...] != 0, 1.0, 0.0).astype(jnp.float32)
    keep = jnp.broadcast_to(keep, (WIDE, rows)).T
    mine = pl.ds(pl.multiple_of(shard * rows, rows), rows)

    def mask(c):
        part = cot[:, c * WIDE : (c + 1) * WIDE].astype(jnp.float32)
        gath[c, mine, :] = jnp.where(keep != 0.0, part, 0.0).astype(jnp.bfloat16)

    cot_load.wait()
    mask(0)

    def gather_copy(c, j):
        peer = lax.rem(shard + j, shards)
        return pltpu.make_async_remote_copy(
            src_ref=gath.at[c, mine, :],
            dst_ref=gath.at[c, mine, :],
            send_sem=gather_send.at[c, j - 1],
            recv_sem=gather_recv.at[c, j - 1],
            device_id=(rep, peer),
            device_id_type=MESH,
        )

    def gather_wait(c):
        for j in range(1, shards):
            peer = lax.rem(shard + shards - j, shards)
            theirs = pl.ds(pl.multiple_of(peer * rows, rows), rows)
            pltpu.make_async_remote_copy(
                src_ref=gath.at[c, theirs, :],
                dst_ref=gath.at[c, theirs, :],
                send_sem=gather_send.at[c, j - 1],
                recv_sem=gather_recv.at[c, j - 1],
                device_id=(rep, peer),
                device_id_type=MESH,
            ).wait_recv()

    def gossip_copy(c, p):
        return pltpu.make_async_remote_copy(
            src_ref=outbox.at[c, p],
            dst_ref=inbox.at[c, p],
            send_sem=gossip_send.at[c, p],
            recv_sem=gossip_recv.at[c, p],
            device_id=(target, shard),
            device_id_type=MESH,
        )

    pl.semaphore_wait(barrier, signals)
    for j in range(1, shards):
        gather_copy(0, j).start()

    for c in range(1, chunks):
        mask(c)
    acts_load.wait()

    @pl.loop(0, pieces)
    def _(p):
        span = pl.ds(pl.multiple_of(p * tall, tall), tall)
        acts_t[span, :] = acts[:, span].T

    for c in range(chunks):
        for j in range(1, shards):
            gather_copy(c, j).wait_send()
            if c + 1 < chunks:
                gather_copy(c + 1, j).start()
        for load in state_loads(c):
            load.wait()
        gather_wait(c)
        columns = slice(c * WIDE, (c + 1) * WIDE)

        @pl.loop(0, pieces)
        def _(p):
            span = pl.ds(pl.multiple_of(p * tall, tall), tall)
            gradient = jnp.dot(
                acts_t[span, :], gath[c], preferred_element_type=jnp.float32
            ) * (1.0 / tokens)
            own = weight[span, columns]
            new_moment = beta_one * moment[span, columns] + (1.0 - beta_one) * gradient
            new_second = beta_two * second[span, columns] + (1.0 - beta_two) * gradient * gradient
            updated = own - learn_rate * (
                new_moment / (jnp.sqrt(new_second) + epsilon) + decay_rate * own
            )
            outbox[c, p, 0] = updated.astype(jnp.bfloat16)
            outbox[c, p, 1] = new_moment.astype(jnp.bfloat16)
            gossip_copy(c, p).start()
            weight_half[span, columns] = own.astype(jnp.bfloat16)
            weight[span, columns] = updated
            moment[span, columns] = new_moment
            second[span, columns] = new_second

    gtall = min(TALL, tokens)

    @pl.loop(0, tokens // gtall)
    def _(t):
        span = pl.ds(pl.multiple_of(t * gtall, gtall), gtall)
        left = jnp.concatenate([gath[c, span, :] for c in range(chunks)], axis=1)
        grad[span, :] = lax.dot_general(
            left, weight_half[...], (((1,), (1,)), ((), ())), preferred_element_type=jnp.float32
        ).astype(jnp.bfloat16)

    for c in range(chunks):
        columns = slice(c * WIDE, (c + 1) * WIDE)

        @pl.loop(0, pieces)
        def _(p):
            span = pl.ds(pl.multiple_of(p * tall, tall), tall)
            gossip_copy(c, p).wait_recv()
            weight[span, columns] = 0.5 * (weight[span, columns] + inbox[c, p, 0].astype(jnp.float32))
            moment[span, columns] = 0.5 * (moment[span, columns] + inbox[c, p, 1].astype(jnp.float32))

    for c in range(chunks):

        @pl.loop(0, pieces)
        def _(p):
            gossip_copy(c, p).wait_send()


def settle(values):
    def write(*refs):
        count = len(values)
        sem = refs[-1]
        copies = []
        for i in range(count):
            rows = values[i].shape[-2] // PARTS
            for part in range(PARTS):
                span = pl.ds(part * rows, rows)
                index = (span, slice(None)) if values[i].ndim == 2 else (0, span, slice(None))
                copies.append(
                    pltpu.make_async_copy(
                        refs[i].at[index], refs[count + i].at[index], sem.at[i, part]
                    )
                )
        for copy in copies:
            copy.start()
        for copy in copies:
            copy.wait()

    return pl.pallas_call(
        write,
        out_shape=tuple(jax.ShapeDtypeStruct(v.shape, v.dtype) for v in values),
        in_specs=[pl.BlockSpec(memory_space=pltpu.VMEM)] * len(values),
        out_specs=(pl.BlockSpec(memory_space=pltpu.HBM),) * len(values),
        scratch_shapes=[pltpu.SemaphoreType.DMA((len(values), PARTS))],
        compiler_params=pltpu.CompilerParams(vmem_limit_bytes=4 * 1024 * 1024),
        name="settle",
    )(*[pltpu.with_memory_space_constraint(v, pltpu.VMEM) for v in values])


def fused(replicas, shards, level, acts, cot, ids, weight, moment, second):
    tokens, feats = acts.shape
    rows, width = cot.shape
    chunks = width // WIDE
    tall = min(TALL, feats)
    pieces = feats // tall
    state = pltpu.VMEM(weight.shape, jnp.float32)
    far = pl.BlockSpec(memory_space=pltpu.HBM)
    values = pl.pallas_call(
        partial(body, replicas, shards, (1 << level) % replicas),
        out_shape=(pltpu.VMEM((tokens, feats), jnp.bfloat16), state, state, state),
        in_specs=[
            far,
            far,
            far,
            far,
            far,
            far,
        ],
        out_specs=(pl.BlockSpec(memory_space=pltpu.VMEM),) * 4,
        scratch_shapes=[
            pltpu.VMEM((tokens, feats), jnp.bfloat16),
            pltpu.VMEM((feats, tokens), jnp.bfloat16),
            pltpu.VMEM((rows, width), jnp.bfloat16),
            pltpu.VMEM((1, rows), jnp.int32),
            pltpu.VMEM((chunks, tokens, WIDE), jnp.bfloat16),
            pltpu.VMEM((feats, width), jnp.bfloat16),
            pltpu.VMEM((chunks, pieces, 2, tall, WIDE), jnp.bfloat16),
            pltpu.VMEM((chunks, pieces, 2, tall, WIDE), jnp.bfloat16),
            pltpu.SemaphoreType.DMA((3,)),
            pltpu.SemaphoreType.DMA((3, chunks)),
            pltpu.SemaphoreType.DMA((chunks, shards - 1)),
            pltpu.SemaphoreType.DMA((chunks, shards - 1)),
            pltpu.SemaphoreType.DMA((chunks, pieces)),
            pltpu.SemaphoreType.DMA((chunks, pieces)),
        ],
        compiler_params=pltpu.CompilerParams(
            collective_id=level, has_side_effects=True, vmem_limit_bytes=32 * 1024 * 1024
        ),
        name=f"gossip_offset_{1 << level}",
    )(acts, cot, ids, weight, moment, second)
    return settle(values)


def on_device(replicas, shards, acts, cot, token_ids, round_index, weight, moment, second):
    levels = max(1, replicas.bit_length() - 1)
    branches = [partial(fused, replicas, shards, level) for level in range(levels)]
    ids = token_ids.reshape(1, -1)
    return lax.switch(round_index, branches, acts, cot, ids, weight, moment, second)


def solution(mesh):
    return jax.shard_map(
        partial(on_device, mesh.shape["rep"], mesh.shape["fsdp"]),
        mesh=mesh,
        in_specs=(
            P("rep", "fsdp"),
            P(("rep", "fsdp"), None),
            P(("rep", "fsdp")),
            P(),
            P("rep", "fsdp", None),
            P("rep", "fsdp", None),
            P("rep", "fsdp", None),
        ),
        out_specs=(
            P("rep", "fsdp"),
            P("rep", "fsdp", None),
            P("rep", "fsdp", None),
            P("rep", "fsdp", None),
        ),
        check_vma=False,
    )
```
